32 devices in a mesh: parts: 2 (over y), tile: 4 (over z), tm: 2 (over x), orb: 2 (over core).
Axes of the slice: x: 2, y: 2, z: 4, core: 2. Of those that a mesh axis runs over, the one named last changes fastest.
Arguments:
- occ_orbitals: bfloat16 [16384, 512], P('tile', ('parts', 'orb')), parts along dimension 1, may hold values from -4 to 4
- occ_tangents: bfloat16 [3, 16384, 512], P(None, 'tile', ('parts', 'orb')), parts along dimension 2, may hold values from -4 to 4
- vir_orbitals: bfloat16 [16384, 4096], P('tile', ('parts', 'orb')), parts along dimension 1, may hold values from -2 to 2
- vir_tangents: bfloat16 [3, 16384, 4096], P(None, 'tile', ('parts', 'orb')), parts along dimension 2, may hold values from -2 to 2
- occ_energy: float32 [512], P(('parts', 'orb')), parts along dimension 0, may hold values from -1 to -0.1
- occ_shift: float32 [3, 512], P(None, ('parts', 'orb')), parts along dimension 1, may hold values from -0.5 to 0.5
- vir_energy: float32 [4096], P(('parts', 'orb')), parts along dimension 0, may hold values from 0.1 to 1.5
- vir_shift: float32 [3, 4096], P(None, ('parts', 'orb')), parts along dimension 1, may hold values from -0.5 to 0.5
- time_index: int32 [2], replicated, may hold values from 0 to 11
- freq_index: int32 [2], replicated, may hold values from 0 to 11
Outputs:
- chi_tangent: bfloat16 [3, 2, 32, 16384], P(None, None, ('parts', 'orb'), ('tile', 'tm')), parts along dimension 2
The draws below stay inside these ranges and needn't reach their ends.
There are 2 independent parts, one for each index of `parts`. The reference program is written for one: setup_inputs(seed, part) draws one part's arguments, and reference() takes and returns one part's arrays. A program takes and returns all parts, laid end to end along the dimension named above; an argument that names none is the same for every part. Nothing has to cross between parts.
All inputs are finite; a program needn't handle non-finite values.
Results may differ from the reference program's by a relative error of at most 0.014.
Values may be sent and summed in bfloat16 or wider, within the bound.
A program may use at most 128 MiB of HBM per device.

```python
import jax
import jax.numpy as jnp
from jax import lax

NAUX = 16384
SLAB_DEV = 4
OCC_DEV = 128
VIR_DEV = 1024
MODES = 3
NT = 2
NF = 2
PSLAB = 16
OCC = 256
VIR = 2048
N_TILE = 4
N_ORB = 2


def steps_of(rng, extent, split, smallest, high):
    factor_of = 1.0
    for axis_at, blocks in split:
        heights = jax.random.uniform(jax.random.fold_in(jax.random.fold_in(rng, 6), axis_at), (blocks,), jnp.float32, smallest / len(split), high / len(split))
        factor_of = factor_of * jnp.repeat(jnp.exp(heights), extent[axis_at] // blocks).reshape((-1,) + (1,) * (len(extent) - 1 - axis_at))
    return factor_of


def normal_values(key, dims, scale, reach, split=(), dtype=jnp.bfloat16):
    result = jax.random.normal(key, dims, jnp.float32) * scale
    if len(split) > 0:
        result = steps_of(key, dims, split, -0.22, 0.18) * result
    return jnp.clip(result, min=-reach, max=reach).astype(dtype)


def setup_inputs(seed: int = 0, part: int = 0) -> dict:
    arg_keys = jax.random.split(jax.random.key(seed), 11)
    part_splits = jax.random.split(jax.random.fold_in(arg_keys[10], part), 11)
    occ_orbitals = normal_values(part_splits[0], (NAUX, OCC), 0.25, 4.0, ((0, 4), (1, 2)))
    occ_tangents = normal_values(part_splits[1], (MODES, NAUX, OCC), 0.25, 4.0, ((1, 4), (2, 2)))
    vir_orbitals = normal_values(part_splits[2], (NAUX, VIR), 0.15, 2.0, ((0, 4), (1, 2)))
    vir_tangents = normal_values(part_splits[3], (MODES, NAUX, VIR), 0.15, 2.0, ((1, 4), (2, 2)))
    occ_energy = jnp.clip(-1.0 + 0.9 * jax.random.uniform(part_splits[4], (OCC,), jnp.float32) ** steps_of(part_splits[4], (OCC,), ((0, 2),), -0.2, 0.2), -1.0, -0.1)
    occ_shift = jnp.clip(jax.random.uniform(part_splits[5], (MODES, OCC), jnp.float32, -0.5, 0.5) * steps_of(part_splits[5], (MODES, OCC), ((1, 2),), -0.4, 0.0), -0.5, 0.5)
    vir_energy = jnp.clip(0.1 + 1.4 * jax.random.uniform(part_splits[6], (VIR,), jnp.float32) ** steps_of(part_splits[6], (VIR,), ((0, 2),), -0.2, 0.2), 0.1, 1.5)
    vir_shift = jnp.clip(jax.random.uniform(part_splits[7], (MODES, VIR), jnp.float32, -0.5, 0.5) * steps_of(part_splits[7], (MODES, VIR), ((1, 2),), -0.4, 0.0), -0.5, 0.5)
    time_index = jax.random.randint(arg_keys[8], (NT,), 0, 12).astype(jnp.int32)
    freq_index = jax.random.randint(arg_keys[9], (NF,), 0, 12).astype(jnp.int32)
    return dict(occ_orbitals=occ_orbitals, occ_tangents=occ_tangents, vir_orbitals=vir_orbitals, vir_tangents=vir_tangents, occ_energy=occ_energy, occ_shift=occ_shift, vir_energy=vir_energy, vir_shift=vir_shift, time_index=time_index, freq_index=freq_index)


def time_grid(time_index, freq_index):
    tau_all = 0.1 * jnp.power(jnp.float32(1.35), time_index.astype(jnp.float32))
    omega_all = 0.2 * jnp.power(jnp.float32(1.4), freq_index.astype(jnp.float32))
    return tau_all, 0.6 * tau_all[None, :] * jnp.cos(omega_all[:, None] * tau_all[None, :])


def slab_of(values):
    lead = values.shape[:-2]
    shaped = values.reshape(lead + (N_TILE, NAUX // N_TILE, values.shape[-1]))[..., :SLAB_DEV, :]
    return shaped.reshape(lead + (N_TILE * SLAB_DEV, values.shape[-1]))


def rounded(values):
    return lax.optimization_barrier(values.astype(jnp.bfloat16)).astype(jnp.float32)


def green_side(orbitals, tangents, weight, weight_tangent, batch_width):
    scaled = (orbitals.astype(jnp.float32) * weight[None, :]).astype(jnp.bfloat16)
    moved = (tangents.astype(jnp.float32) * weight[None, None, :]
             + orbitals.astype(jnp.float32)[None] * weight_tangent[:, None, :]).astype(jnp.bfloat16)
    slab_left = slab_of(orbitals)
    slab_tangent = slab_of(tangents)
    green = jnp.zeros((slab_left.shape[0], NAUX), jnp.float32)
    change = jnp.zeros((MODES, slab_left.shape[0], NAUX), jnp.float32)
    for batch in range(N_ORB):
        low = batch * batch_width
        high = low + batch_width
        part_green = jnp.dot(slab_left[:, low:high], scaled[:, low:high].T, preferred_element_type=jnp.float32)
        part_change = jnp.einsum('mso,qo->msq', slab_tangent[..., low:high].astype(jnp.float32),
                                 scaled[:, low:high].astype(jnp.float32))
        part_change = part_change + jnp.einsum('so,mqo->msq', slab_left[:, low:high].astype(jnp.float32),
                                               moved[..., low:high].astype(jnp.float32))
        green = green + rounded(part_green)
        change = change + rounded(part_change)
    return green, change


def reference(occ_orbitals, occ_tangents, vir_orbitals, vir_tangents, occ_energy, occ_shift,
              vir_energy, vir_shift, time_index, freq_index):
    tau_all, weights = time_grid(time_index, freq_index)
    running = jnp.zeros((MODES, NF, PSLAB, NAUX), jnp.float32)
    for step in range(NT):
        tau_now = tau_all[step]
        occ_weight = jnp.exp(occ_energy * tau_now)
        occ_change = tau_now * occ_shift * occ_weight[None, :]
        vir_weight = jnp.exp(-vir_energy * tau_now)
        vir_change = -tau_now * vir_shift * vir_weight[None, :]
        green_occ, dgreen_occ = green_side(occ_orbitals, occ_tangents, occ_weight, occ_change, OCC_DEV)
        green_vir, dgreen_vir = green_side(vir_orbitals, vir_tangents, vir_weight, vir_change, VIR_DEV)
        chi_tau = (dgreen_occ * green_vir[None] + green_occ[None] * dgreen_vir).astype(jnp.bfloat16)
        term = weights[:, step][None, :, None, None] * chi_tau.astype(jnp.float32)[:, None]
        running = running + rounded(term)
    return running.astype(jnp.bfloat16)
```

```python
import functools
import math

import jax
import jax.numpy as jnp
from jax import lax
from jax.experimental import pallas as pl
from jax.experimental.pallas import tpu as pltpu
from jax.sharding import PartitionSpec as P

SLAB_DEV = 4
CHUNK = 512
MESH = pl.DeviceIdType.MESH
F32 = jnp.float32
BF16 = jnp.bfloat16


def dot_nt(left, points):
    return lax.dot_general(left, points, (((1,), (1,)), ((), ())), preferred_element_type=F32)


def kernel(
    n_tile,
    chunk,
    time_ref,
    freq_ref,
    occ_hbm,
    occ_t_hbm,
    vir_hbm,
    vir_t_hbm,
    occ_e,
    occ_s,
    vir_e,
    vir_s,
    out_ref,
    x_occ,
    x_vir,
    head_occ,
    head_vir,
    pack,
    gathered,
    slab,
    left_occ,
    left_vir,
    left0_occ,
    left0_vir,
    mine,
    outgoing,
    incoming,
    load_sem,
    head_sem,
    tile_send,
    tile_recv,
    orb_send,
    orb_recv,
):
    n_modes = occ_t_hbm.shape[0]
    groups = 1 + n_modes
    n_occ = occ_hbm.shape[1]
    n_vir = vir_hbm.shape[1]
    n_time = time_ref.shape[0]
    n_freq = freq_ref.shape[0]
    points = x_vir.shape[1]
    n_chunk = points // chunk
    rows = out_ref.shape[2]
    half = n_time * groups * rows
    me = lax.axis_index("tile")
    orb = lax.axis_index("orb")
    other = 1 - orb
    first = pl.multiple_of(lax.axis_index("tm") * points, points)

    heads = [
        pltpu.make_async_copy(occ_hbm.at[pl.ds(0, 16)], head_occ.at[0], head_sem.at[0]),
        pltpu.make_async_copy(occ_t_hbm.at[:, pl.ds(0, 16)], head_occ.at[pl.ds(1, n_modes)], head_sem.at[1]),
        pltpu.make_async_copy(vir_hbm.at[pl.ds(0, 16)], head_vir.at[0], head_sem.at[2]),
        pltpu.make_async_copy(vir_t_hbm.at[:, pl.ds(0, 16)], head_vir.at[pl.ds(1, n_modes)], head_sem.at[3]),
    ]
    for copy in heads:
        copy.start()

    barrier = pltpu.get_barrier_semaphore()
    for off in range(1, n_tile):
        pl.semaphore_signal(
            barrier, inc=1, device_id={"tile": lax.rem(me + off, n_tile)}, device_id_type=MESH
        )
    pl.semaphore_signal(barrier, inc=1, device_id={"orb": other}, device_id_type=MESH)

    loads = []
    for i in range(n_chunk):
        src = pl.ds(first + i * chunk, chunk)
        dst = pl.ds(i * chunk, chunk)
        loads.append([
            pltpu.make_async_copy(vir_hbm.at[src], x_vir.at[0, dst], load_sem.at[i, 0]),
            pltpu.make_async_copy(vir_t_hbm.at[:, src], x_vir.at[pl.ds(1, n_modes), dst], load_sem.at[i, 1]),
            pltpu.make_async_copy(occ_hbm.at[src], x_occ.at[0, dst], load_sem.at[i, 2]),
            pltpu.make_async_copy(occ_t_hbm.at[:, src], x_occ.at[pl.ds(1, n_modes), dst], load_sem.at[i, 3]),
        ])
        for copy in loads[i]:
            copy.start()

    for copy in heads:
        copy.wait()
    for g in range(groups):
        at = pl.ds(g * SLAB_DEV, SLAB_DEV)
        pack[at, :n_occ] = head_occ[g].astype(F32)[:SLAB_DEV]
        pack[at, n_occ:] = head_vir[g].astype(F32)[:SLAB_DEV]
    gathered[me] = pack[...].astype(BF16)

    pl.semaphore_wait(barrier, n_tile)
    sends = []
    for off in range(1, n_tile):
        copy = pltpu.make_async_remote_copy(
            src_ref=gathered.at[me],
            dst_ref=gathered.at[me],
            send_sem=tile_send.at[off - 1],
            recv_sem=tile_recv.at[off - 1],
            device_id={"tile": lax.rem(me + off, n_tile)},
            device_id_type=MESH,
        )
        copy.start()
        sends.append(copy)

    def tau_of(j, width):
        return 0.1 * jnp.exp(jnp.full((1, width), time_ref[j].astype(F32) * math.log(1.35), F32))

    occ_w, occ_dw, vir_w, vir_dw, freq_w = [], [], [], [], []
    for j in range(n_time):
        tau = tau_of(j, n_occ)
        weight = jnp.exp(occ_e[...].reshape(1, n_occ) * tau)
        occ_w.append(weight)
        occ_dw.append(tau * occ_s[...] * weight)
        tau = tau_of(j, n_vir)
        weight = jnp.exp(-vir_e[...].reshape(1, n_vir) * tau)
        vir_w.append(weight)
        vir_dw.append(-tau * vir_s[...] * weight)
        tau = tau_of(j, 128)
        column = []
        for k in range(n_freq):
            omega = 0.2 * jnp.exp(jnp.full((1, 128), freq_ref[k].astype(F32) * math.log(1.4), F32))
            w = 0.6 * tau * jnp.cos(omega * tau)
            column.append(jnp.concatenate([w] * (chunk // 128), axis=1))
        freq_w.append(column)

    for copy in sends:
        copy.wait_recv()

    for d in range(n_tile):
        block = gathered[d].astype(F32)
        for g in range(groups):
            slab[g, pl.ds(d * SLAB_DEV, SLAB_DEV)] = block[g * SLAB_DEV : (g + 1) * SLAB_DEV]
    for h, start in enumerate((orb, other)):
        at = pl.ds(pl.multiple_of(start * rows, rows), rows)
        for cols, width, weight, change, left, left0 in (
            (pl.ds(0, n_occ), n_occ, occ_w, occ_dw, left_occ, left0_occ),
            (pl.ds(n_occ, n_vir), n_vir, vir_w, vir_dw, left_vir, left0_vir),
        ):
            base = slab[0, at, cols]
            tangent = [slab[1 + m, at, cols] for m in range(n_modes)]
            zeroth = []
            full = []
            for j in range(n_time):
                scaled = base * weight[j]
                zeroth.append(scaled)
                full.append(scaled)
                for m in range(n_modes):
                    full.append(tangent[m] * weight[j] + base * change[j][m : m + 1])
            left[pl.ds(h * half, half)] = jnp.concatenate(full, axis=0).astype(BF16)
            left0[pl.ds(h * n_time * rows, n_time * rows)] = jnp.concatenate(zeroth, axis=0).astype(BF16)

    def exchange(i):
        return pltpu.make_async_remote_copy(
            src_ref=outgoing.at[i],
            dst_ref=incoming.at[i],
            send_sem=orb_send.at[i],
            recv_sem=orb_recv.at[i],
            device_id={"orb": other},
            device_id_type=MESH,
        )

    def partial(i):
        at = pl.ds(i * chunk, chunk)
        for copy in loads[i]:
            copy.wait()
        for side, (x, left, left0) in enumerate(
            ((x_occ, left_occ, left0_occ), (x_vir, left_vir, left0_vir))
        ):
            total = dot_nt(left[...], x[0, at])
            moved = [dot_nt(left0[...], x[1 + m, at]) for m in range(n_modes)]
            for h in range(2):
                parts = []
                for j in range(n_time):
                    for g in range(groups):
                        low = h * half + (j * groups + g) * rows
                        value = total[low : low + rows]
                        if g > 0:
                            low = (h * n_time + j) * rows
                            value = value + moved[g - 1][low : low + rows]
                        parts.append(value)
                value = jnp.concatenate(parts, axis=0)
                if h == 0:
                    mine[i, side] = value
                else:
                    outgoing[i, side] = value.astype(BF16)
        copy = exchange(i)
        copy.start()
        return copy

    def finish(i):
        at = pl.ds(i * chunk, chunk)
        green = [mine[i, side] + incoming[i, side].astype(F32) for side in range(2)]

        def pick(side, j, g):
            low = (j * groups + g) * rows
            return green[side][low : low + rows]

        for m in range(n_modes):
            chi = [
                (pick(0, j, 1 + m) * pick(1, j, 0) + pick(0, j, 0) * pick(1, j, 1 + m))
                .astype(BF16)
                .astype(F32)
                for j in range(n_time)
            ]
            for k in range(n_freq):
                total = None
                for j in range(n_time):
                    term = (freq_w[j][k] * chi[j]).astype(BF16).astype(F32)
                    total = term if total is None else total + term
                out_ref[m, k, :, at] = total.astype(BF16)

    copies = []
    for i in range(n_chunk):
        copies.append(partial(i))
        if i > 0:
            copies[i - 1].wait_recv()
            finish(i - 1)
    copies[n_chunk - 1].wait_recv()
    finish(n_chunk - 1)
    for copy in sends + copies:
        copy.wait_send()


def shards(mesh, *args):
    (occ, occ_t, vir, vir_t, occ_e, occ_s, vir_e, vir_s, time_index, freq_index) = args
    n_tile, n_tm, n_orb = mesh.shape["tile"], mesh.shape["tm"], mesh.shape["orb"]
    n_modes = occ_t.shape[0]
    groups = 1 + n_modes
    n_occ, n_vir = occ.shape[1], vir.shape[1]
    n_time, n_freq = time_index.shape[0], freq_index.shape[0]
    points = occ.shape[0] // n_tm
    chunk = min(CHUNK, points)
    n_chunk = points // chunk
    slab_rows = n_tile * SLAB_DEV
    rows = slab_rows // n_orb
    left_rows = n_time * groups * slab_rows
    half = left_rows // n_orb
    hbm = pl.BlockSpec(memory_space=pltpu.HBM)
    vmem = pl.BlockSpec(memory_space=pltpu.VMEM)
    smem = pl.BlockSpec(memory_space=pltpu.SMEM)
    dma = pltpu.SemaphoreType.DMA
    return pl.pallas_call(
        functools.partial(kernel, n_tile, chunk),
        out_shape=jax.ShapeDtypeStruct((n_modes, n_freq, rows, points), BF16),
        in_specs=[smem] * 2 + [hbm] * 4 + [vmem] * 4,
        out_specs=vmem,
        scratch_shapes=[
            pltpu.VMEM((groups, points, n_occ), BF16),
            pltpu.VMEM((groups, points, n_vir), BF16),
            pltpu.VMEM((groups, 16, n_occ), BF16),
            pltpu.VMEM((groups, 16, n_vir), BF16),
            pltpu.VMEM((groups * SLAB_DEV, n_occ + n_vir), F32),
            pltpu.VMEM((n_tile, groups * SLAB_DEV, n_occ + n_vir), BF16),
            pltpu.VMEM((groups, slab_rows, n_occ + n_vir), F32),
            pltpu.VMEM((left_rows, n_occ), BF16),
            pltpu.VMEM((left_rows, n_vir), BF16),
            pltpu.VMEM((n_time * slab_rows, n_occ), BF16),
            pltpu.VMEM((n_time * slab_rows, n_vir), BF16),
            pltpu.VMEM((n_chunk, 2, half, chunk), F32),
            pltpu.VMEM((n_chunk, 2, half, chunk), BF16),
            pltpu.VMEM((n_chunk, 2, half, chunk), BF16),
            dma((n_chunk, 4)),
            dma((4,)),
            dma((n_tile - 1,)),
            dma((n_tile - 1,)),
            dma((n_chunk,)),
            dma((n_chunk,)),
        ],
        compiler_params=pltpu.CompilerParams(
            collective_id=0, has_side_effects=True, vmem_limit_bytes=56 * 1024 * 1024
        ),
        name="polarizability_tangent",
    )(time_index, freq_index, occ, occ_t, vir, vir_t, occ_e, occ_s, vir_e, vir_s)


def solution(mesh):
    in_specs = (
        P("tile", ("parts", "orb")),
        P(None, "tile", ("parts", "orb")),
        P("tile", ("parts", "orb")),
        P(None, "tile", ("parts", "orb")),
        P(("parts", "orb")),
        P(None, ("parts", "orb")),
        P(("parts", "orb")),
        P(None, ("parts", "orb")),
        P(),
        P(),
    )
    out_specs = P(None, None, ("parts", "orb"), ("tile", "tm"))
    return jax.shard_map(
        functools.partial(shards, mesh),
        mesh=mesh,
        in_specs=in_specs,
        out_specs=out_specs,
        check_vma=False,
    )
```

```python
import functools
import math

import jax
import jax.numpy as jnp
from jax import lax
from jax.experimental import pallas as pl
from jax.experimental.pallas import tpu as pltpu
from jax.sharding import PartitionSpec as P

SLAB_DEV = 4
CHUNKS = (512, 512, 512, 512)
MESH = pl.DeviceIdType.MESH
F32 = jnp.float32
BF16 = jnp.bfloat16


def dot_nt(left, points):
    return lax.dot_general(left, points, (((1,), (1,)), ((), ())), preferred_element_type=F32)


def kernel(
    n_tile,
    chunks,
    time_hbm,
    freq_hbm,
    occ_hbm,
    occ_t_hbm,
    vir_hbm,
    vir_t_hbm,
    occ_e_hbm,
    occ_s_hbm,
    vir_e_hbm,
    vir_s_hbm,
    out_ref,
    time_ref,
    freq_ref,
    occ_e,
    occ_s,
    vir_e,
    vir_s,
    weights,
    columns,
    x_occ,
    x_vir,
    head_occ,
    head_vir,
    pack,
    gathered,
    slab,
    left_occ,
    left_vir,
    left0_vir,
    mine,
    outgoing,
    incoming,
    load_sem,
    head_sem,
    small_sem,
    tile_send,
    tile_recv,
    orb_send,
    orb_recv,
):
    n_modes = occ_t_hbm.shape[0]
    groups = 1 + n_modes
    n_occ = occ_hbm.shape[1]
    n_vir = vir_hbm.shape[1]
    n_time = time_ref.shape[0]
    n_freq = freq_ref.shape[0]
    points = x_vir.shape[1]
    n_chunk = len(chunks)
    starts = [sum(chunks[:i]) for i in range(n_chunk)]
    rows = out_ref.shape[2]
    half = n_time * groups * rows
    me = lax.axis_index("tile")
    orb = lax.axis_index("orb")
    other = 1 - orb
    first = pl.multiple_of(lax.axis_index("tm") * points, points)

    heads = [
        pltpu.make_async_copy(occ_hbm.at[pl.ds(0, 16)], head_occ.at[0], head_sem.at[0]),
        pltpu.make_async_copy(occ_t_hbm.at[:, pl.ds(0, 16)], head_occ.at[pl.ds(1, n_modes)], head_sem.at[1]),
        pltpu.make_async_copy(vir_hbm.at[pl.ds(0, 16)], head_vir.at[0], head_sem.at[2]),
        pltpu.make_async_copy(vir_t_hbm.at[:, pl.ds(0, 16)], head_vir.at[pl.ds(1, n_modes)], head_sem.at[3]),
    ]
    for copy in heads:
        copy.start()

    barrier = pltpu.get_barrier_semaphore()
    for off in range(1, n_tile):
        pl.semaphore_signal(
            barrier, inc=1, device_id={"tile": lax.rem(me + off, n_tile)}, device_id_type=MESH
        )
    pl.semaphore_signal(barrier, inc=1, device_id={"orb": other}, device_id_type=MESH)

    smalls = [
        pltpu.make_async_copy(src, dst, small_sem.at[at])
        for at, (src, dst) in enumerate((
            (time_hbm, time_ref),
            (freq_hbm, freq_ref),
            (occ_e_hbm, occ_e),
            (occ_s_hbm, occ_s),
            (vir_e_hbm, vir_e),
            (vir_s_hbm, vir_s),
        ))
    ]
    for copy in smalls:
        copy.start()
    loads = []
    for i in range(n_chunk):
        src = pl.ds(first + starts[i], chunks[i])
        dst = pl.ds(starts[i], chunks[i])
        loads.append([
            pltpu.make_async_copy(vir_hbm.at[src], x_vir.at[0, dst], load_sem.at[i, 0]),
            pltpu.make_async_copy(vir_t_hbm.at[:, src], x_vir.at[pl.ds(1, n_modes), dst], load_sem.at[i, 1]),
            pltpu.make_async_copy(occ_hbm.at[src], x_occ.at[0, dst], load_sem.at[i, 2]),
            pltpu.make_async_copy(occ_t_hbm.at[:, src], x_occ.at[pl.ds(1, n_modes), dst], load_sem.at[i, 3]),
        ])
        for copy in loads[i]:
            copy.start()

    for copy in heads:
        copy.wait()
    for g in range(groups):
        at = pl.ds(g * SLAB_DEV, SLAB_DEV)
        pack[at, :n_occ] = head_occ[g].astype(F32)[:SLAB_DEV]
        pack[at, n_occ:] = head_vir[g].astype(F32)[:SLAB_DEV]
    gathered[me] = pack[...].astype(BF16)

    pl.semaphore_wait(barrier, n_tile)
    sends = []
    for off in range(1, n_tile):
        copy = pltpu.make_async_remote_copy(
            src_ref=gathered.at[me],
            dst_ref=gathered.at[me],
            send_sem=tile_send.at[off - 1],
            recv_sem=tile_recv.at[off - 1],
            device_id={"tile": lax.rem(me + off, n_tile)},
            device_id_type=MESH,
        )
        copy.start()
        sends.append(copy)

    def tau_of(j, width):
        return 0.1 * jnp.exp(jnp.full((1, width), time_ref[j].astype(F32) * math.log(1.35), F32))

    for copy in smalls:
        copy.wait()
    occ_cols, vir_cols = pl.ds(0, n_occ), pl.ds(n_occ, n_vir)
    for j in range(n_time):
        for cols, width, energy, shift, sign in (
            (occ_cols, n_occ, occ_e, occ_s, 1.0),
            (vir_cols, n_vir, vir_e, vir_s, -1.0),
        ):
            tau = sign * tau_of(j, width)
            weight = jnp.exp(energy[...].reshape(1, width) * tau)
            weights[j, pl.ds(0, 1), cols] = weight
            weights[j, pl.ds(1, n_modes), cols] = tau * shift[...] * weight
        tau = tau_of(j, 128)
        for k in range(n_freq):
            omega = 0.2 * jnp.exp(jnp.full((1, 128), freq_ref[k].astype(F32) * math.log(1.4), F32))
            columns[j, pl.ds(k, 1)] = 0.6 * tau * jnp.cos(omega * tau)

    for i in range(n_chunk):
        for copy in loads[i]:
            copy.wait()
    for copy in sends:
        copy.wait_recv()

    for d in range(n_tile):
        block = gathered[d].astype(F32)
        for g in range(groups):
            slab[g, pl.ds(d * SLAB_DEV, SLAB_DEV)] = block[g * SLAB_DEV : (g + 1) * SLAB_DEV]
    for h, start in enumerate((orb, other)):
        at = pl.ds(pl.multiple_of(start * rows, rows), rows)
        for cols, width, left in ((occ_cols, n_occ, left_occ), (vir_cols, n_vir, left_vir)):
            base = slab[0, at, cols]
            tangent = [slab[1 + m, at, cols] for m in range(n_modes)]
            zero = jnp.zeros_like(base)
            zeroth = []
            full = []
            for j in range(n_time):
                weight = weights[j, pl.ds(0, 1), cols]
                zeroth.append(base * weight)
                full.append(zeroth[j])
                for m in range(n_modes):
                    full.append(tangent[m] * weight + base * weights[j, pl.ds(1 + m, 1), cols])
            left[pl.ds(h * half, half), pl.ds(0, width)] = jnp.concatenate(full, axis=0).astype(BF16)
            if left is left_vir:
                value = jnp.concatenate(zeroth, axis=0).astype(BF16)
                left0_vir[pl.ds(h * n_time * rows, n_time * rows)] = value
                continue
            for g in range(1, groups):
                full = [zeroth[j] if g == at_g else zero for j in range(n_time) for at_g in range(groups)]
                value = jnp.concatenate(full, axis=0).astype(BF16)
                left[pl.ds(h * half, half), pl.ds(g * width, width)] = value

    def exchange(i):
        return pltpu.make_async_remote_copy(
            src_ref=outgoing.at[:, :, pl.ds(starts[i], chunks[i])],
            dst_ref=incoming.at[:, :, pl.ds(starts[i], chunks[i])],
            send_sem=orb_send.at[i],
            recv_sem=orb_recv.at[i],
            device_id={"orb": other},
            device_id_type=MESH,
        )

    def partial(i):
        at = pl.ds(starts[i], chunks[i])
        joined = jnp.concatenate([x_occ[g, at] for g in range(groups)], axis=1)
        value = dot_nt(left_occ[...], joined)
        mine[0, :, at] = value[:half]
        outgoing[0, :, at] = value[half:].astype(BF16)
        total = dot_nt(left_vir[...], x_vir[0, at])
        moved = [dot_nt(left0_vir[...], x_vir[1 + m, at]) for m in range(n_modes)]
        for h in range(2):
            parts = []
            for j in range(n_time):
                for g in range(groups):
                    low = h * half + (j * groups + g) * rows
                    value = total[low : low + rows]
                    if g > 0:
                        low = (h * n_time + j) * rows
                        value = value + moved[g - 1][low : low + rows]
                    parts.append(value)
            value = jnp.concatenate(parts, axis=0)
            if h == 0:
                mine[1, :, at] = value
            else:
                outgoing[1, :, at] = value.astype(BF16)
        copy = exchange(i)
        copy.start()
        return copy

    def finish(i):
        at = pl.ds(starts[i], chunks[i])
        green = [mine[side, :, at] + incoming[side, :, at].astype(F32) for side in range(2)]

        def pick(side, j, g):
            low = (j * groups + g) * rows
            return green[side][low : low + rows]

        for m in range(n_modes):
            chi = [
                (pick(0, j, 1 + m) * pick(1, j, 0) + pick(0, j, 0) * pick(1, j, 1 + m))
                .astype(BF16)
                .astype(F32)
                for j in range(n_time)
            ]
            for k in range(n_freq):
                total = None
                for j in range(n_time):
                    column = jnp.concatenate([columns[j, pl.ds(k, 1)]] * (chunks[i] // 128), axis=1)
                    term = (column * chi[j]).astype(BF16).astype(F32)
                    total = term if total is None else total + term
                out_ref[m, k, :, at] = total.astype(BF16)

    copies = []
    for i in range(n_chunk):
        copies.append(partial(i))
        if i > 0:
            copies[i - 1].wait_recv()
            finish(i - 1)
    copies[n_chunk - 1].wait_recv()
    finish(n_chunk - 1)
    for copy in sends + copies:
        copy.wait_send()


def shards(mesh, *args):
    (occ, occ_t, vir, vir_t, occ_e, occ_s, vir_e, vir_s, time_index, freq_index) = args
    n_tile, n_tm, n_orb = mesh.shape["tile"], mesh.shape["tm"], mesh.shape["orb"]
    n_modes = occ_t.shape[0]
    groups = 1 + n_modes
    n_occ, n_vir = occ.shape[1], vir.shape[1]
    n_time, n_freq = time_index.shape[0], freq_index.shape[0]
    points = occ.shape[0] // n_tm
    chunks = CHUNKS if points == sum(CHUNKS) else (points,)
    n_chunk = len(chunks)
    slab_rows = n_tile * SLAB_DEV
    rows = slab_rows // n_orb
    left_rows = n_time * groups * slab_rows
    half = left_rows // n_orb
    hbm = pl.BlockSpec(memory_space=pltpu.HBM)
    vmem = pl.BlockSpec(memory_space=pltpu.VMEM)
    smem = pltpu.SMEM
    dma = pltpu.SemaphoreType.DMA
    return pl.pallas_call(
        functools.partial(kernel, n_tile, chunks),
        out_shape=jax.ShapeDtypeStruct((n_modes, n_freq, rows, points), BF16),
        in_specs=[hbm] * 10,
        out_specs=vmem,
        scratch_shapes=[
            smem((n_time,), jnp.int32),
            smem((n_freq,), jnp.int32),
            pltpu.VMEM((n_occ,), F32),
            pltpu.VMEM((n_modes, n_occ), F32),
            pltpu.VMEM((n_vir,), F32),
            pltpu.VMEM((n_modes, n_vir), F32),
            pltpu.VMEM((n_time, groups, n_occ + n_vir), F32),
            pltpu.VMEM((n_time, n_freq, 128), F32),
            pltpu.VMEM((groups, points, n_occ), BF16),
            pltpu.VMEM((groups, points, n_vir), BF16),
            pltpu.VMEM((groups, 16, n_occ), BF16),
            pltpu.VMEM((groups, 16, n_vir), BF16),
            pltpu.VMEM((groups * SLAB_DEV, n_occ + n_vir), F32),
            pltpu.VMEM((n_tile, groups * SLAB_DEV, n_occ + n_vir), BF16),
            pltpu.VMEM((groups, slab_rows, n_occ + n_vir), F32),
            pltpu.VMEM((left_rows, groups * n_occ), BF16),
            pltpu.VMEM((left_rows, n_vir), BF16),
            pltpu.VMEM((n_time * slab_rows, n_vir), BF16),
            pltpu.VMEM((2, half, points), F32),
            pltpu.VMEM((2, half, points), BF16),
            pltpu.VMEM((2, half, points), BF16),
            dma((n_chunk, 4)),
            dma((4,)),
            dma((6,)),
            dma((n_tile - 1,)),
            dma((n_tile - 1,)),
            dma((n_chunk,)),
            dma((n_chunk,)),
        ],
        compiler_params=pltpu.CompilerParams(
            collective_id=0, has_side_effects=True, vmem_limit_bytes=56 * 1024 * 1024
        ),
        name="polarizability_tangent",
    )(time_index, freq_index, occ, occ_t, vir, vir_t, occ_e, occ_s, vir_e, vir_s)


def solution(mesh):
    in_specs = (
        P("tile", ("parts", "orb")),
        P(None, "tile", ("parts", "orb")),
        P("tile", ("parts", "orb")),
        P(None, "tile", ("parts", "orb")),
        P(("parts", "orb")),
        P(None, ("parts", "orb")),
        P(("parts", "orb")),
        P(None, ("parts", "orb")),
        P(),
        P(),
    )
    out_specs = P(None, None, ("parts", "orb"), ("tile", "tm"))
    return jax.shard_map(
        functools.partial(shards, mesh),
        mesh=mesh,
        in_specs=in_specs,
        out_specs=out_specs,
        check_vma=False,
    )
```

```python
import functools
import math

import jax
import jax.numpy as jnp
from jax import lax
from jax.experimental import pallas as pl
from jax.experimental.pallas import tpu as pltpu
from jax.sharding import PartitionSpec as P

SLAB_DEV = 4
CHUNKS = (2048,)
MESH = pl.DeviceIdType.MESH
F32 = jnp.float32
BF16 = jnp.bfloat16


def dot_nt(left, points):
    return lax.dot_general(left, points, (((1,), (1,)), ((), ())), preferred_element_type=F32)


def kernel(
    n_tile,
    chunks,
    time_hbm,
    freq_hbm,
    occ_hbm,
    occ_t_hbm,
    vir_hbm,
    vir_t_hbm,
    occ_e_hbm,
    occ_s_hbm,
    vir_e_hbm,
    vir_s_hbm,
    out_ref,
    time_ref,
    freq_ref,
    occ_e,
    occ_s,
    vir_e,
    vir_s,
    weights,
    columns,
    x_occ,
    x_vir,
    head_occ,
    head_vir,
    pack,
    gathered,
    slab,
    left_occ,
    left_vir,
    mine,
    outgoing,
    incoming,
    load_sem,
    head_sem,
    small_sem,
    tile_send,
    tile_recv,
    orb_send,
    orb_recv,
):
    n_modes = occ_t_hbm.shape[0]
    groups = 1 + n_modes
    n_occ = occ_hbm.shape[1]
    n_vir = vir_hbm.shape[1]
    n_time = time_ref.shape[0]
    n_freq = freq_ref.shape[0]
    points = x_vir.shape[1]
    n_chunk = len(chunks)
    starts = [sum(chunks[:i]) for i in range(n_chunk)]
    rows = out_ref.shape[2]
    half = n_time * groups * rows
    me = lax.axis_index("tile")
    orb = lax.axis_index("orb")
    other = 1 - orb
    first = pl.multiple_of(lax.axis_index("tm") * points, points)

    barrier = pltpu.get_barrier_semaphore()
    for off in range(1, n_tile):
        pl.semaphore_signal(
            barrier, inc=1, device_id={"tile": lax.rem(me + off, n_tile)}, device_id_type=MESH
        )
    pl.semaphore_signal(barrier, inc=1, device_id={"orb": other}, device_id_type=MESH)

    heads = [
        pltpu.make_async_copy(occ_hbm.at[pl.ds(0, 16)], head_occ.at[0], head_sem.at[0]),
        pltpu.make_async_copy(occ_t_hbm.at[:, pl.ds(0, 16)], head_occ.at[pl.ds(1, n_modes)], head_sem.at[1]),
        pltpu.make_async_copy(vir_hbm.at[pl.ds(0, 16)], head_vir.at[0], head_sem.at[2]),
        pltpu.make_async_copy(vir_t_hbm.at[:, pl.ds(0, 16)], head_vir.at[pl.ds(1, n_modes)], head_sem.at[3]),
    ]
    for copy in heads:
        copy.start()

    smalls = [
        pltpu.make_async_copy(src, dst, small_sem.at[at])
        for at, (src, dst) in enumerate((
            (time_hbm, time_ref),
            (freq_hbm, freq_ref),
            (occ_e_hbm, occ_e),
            (occ_s_hbm, occ_s),
            (vir_e_hbm, vir_e),
            (vir_s_hbm, vir_s),
        ))
    ]
    for copy in smalls:
        copy.start()
    loads = []
    for i in range(n_chunk):
        src = pl.ds(first + starts[i], chunks[i])
        dst = pl.ds(starts[i], chunks[i])
        loads.append([
            pltpu.make_async_copy(vir_hbm.at[src], x_vir.at[0, dst], load_sem.at[i, 0]),
            pltpu.make_async_copy(vir_t_hbm.at[:, src], x_vir.at[pl.ds(1, n_modes), dst], load_sem.at[i, 1]),
            pltpu.make_async_copy(occ_hbm.at[src], x_occ.at[0, dst], load_sem.at[i, 2]),
            pltpu.make_async_copy(occ_t_hbm.at[:, src], x_occ.at[pl.ds(1, n_modes), dst], load_sem.at[i, 3]),
        ])
    for copy in heads:
        copy.wait()
    for i in range(n_chunk):
        for copy in loads[i]:
            copy.start()
    for g in range(groups):
        at = pl.ds(g * SLAB_DEV, SLAB_DEV)
        pack[at, :n_occ] = head_occ[g].astype(F32)[:SLAB_DEV]
        pack[at, n_occ:] = head_vir[g].astype(F32)[:SLAB_DEV]
    gathered[me] = pack[...].astype(BF16)

    pl.semaphore_wait(barrier, n_tile)
    sends = []
    for off in range(1, n_tile):
        copy = pltpu.make_async_remote_copy(
            src_ref=gathered.at[me],
            dst_ref=gathered.at[me],
            send_sem=tile_send.at[off - 1],
            recv_sem=tile_recv.at[off - 1],
            device_id={"tile": lax.rem(me + off, n_tile)},
            device_id_type=MESH,
        )
        copy.start()
        sends.append(copy)

    def tau_of(j, width):
        return 0.1 * jnp.exp(jnp.full((1, width), time_ref[j].astype(F32) * math.log(1.35), F32))

    for copy in smalls:
        copy.wait()
    occ_cols, vir_cols = pl.ds(0, n_occ), pl.ds(n_occ, n_vir)
    for j in range(n_time):
        for cols, width, energy, shift, sign in (
            (occ_cols, n_occ, occ_e, occ_s, 1.0),
            (vir_cols, n_vir, vir_e, vir_s, -1.0),
        ):
            tau = sign * tau_of(j, width)
            weight = jnp.exp(energy[...].reshape(1, width) * tau)
            weights[j, pl.ds(0, 1), cols] = weight
            weights[j, pl.ds(1, n_modes), cols] = tau * shift[...] * weight
        tau = tau_of(j, 128)
        for k in range(n_freq):
            omega = 0.2 * jnp.exp(jnp.full((1, 128), freq_ref[k].astype(F32) * math.log(1.4), F32))
            columns[j, pl.ds(k, 1)] = 0.6 * tau * jnp.cos(omega * tau)

    for i in range(n_chunk):
        for copy in loads[i]:
            copy.wait()
    for copy in sends:
        copy.wait_recv()

    for d in range(n_tile):
        block = gathered[d].astype(F32)
        for g in range(groups):
            slab[g, pl.ds(d * SLAB_DEV, SLAB_DEV)] = block[g * SLAB_DEV : (g + 1) * SLAB_DEV]
    for h, start in enumerate((orb, other)):
        at = pl.ds(pl.multiple_of(start * rows, rows), rows)
        for cols, width, left in ((occ_cols, n_occ, left_occ), (vir_cols, n_vir, left_vir)):
            base = slab[0, at, cols]
            tangent = [slab[1 + m, at, cols] for m in range(n_modes)]
            zero = jnp.zeros_like(base)
            zeroth = []
            full = []
            for j in range(n_time):
                weight = weights[j, pl.ds(0, 1), cols]
                zeroth.append(base * weight)
                full.append(zeroth[j])
                for m in range(n_modes):
                    full.append(tangent[m] * weight + base * weights[j, pl.ds(1 + m, 1), cols])
            left[pl.ds(h * half, half), pl.ds(0, width)] = jnp.concatenate(full, axis=0).astype(BF16)
            for g in range(1, groups):
                full = [zeroth[j] if g == at_g else zero for j in range(n_time) for at_g in range(groups)]
                value = jnp.concatenate(full, axis=0).astype(BF16)
                left[pl.ds(h * half, half), pl.ds(g * width, width)] = value

    def exchange(i):
        return pltpu.make_async_remote_copy(
            src_ref=outgoing.at[:, :, pl.ds(starts[i], chunks[i])],
            dst_ref=incoming.at[:, :, pl.ds(starts[i], chunks[i])],
            send_sem=orb_send.at[i],
            recv_sem=orb_recv.at[i],
            device_id={"orb": other},
            device_id_type=MESH,
        )

    def partial(i):
        at = pl.ds(starts[i], chunks[i])
        for side, (x, left) in enumerate(((x_occ, left_occ), (x_vir, left_vir))):
            joined = jnp.concatenate([x[g, at] for g in range(groups)], axis=1)
            value = dot_nt(joined, left[...]).T
            mine[side, :, at] = value[:half]
            outgoing[side, :, at] = value[half:].astype(BF16)
        copy = exchange(i)
        copy.start()
        return copy

    def finish(i):
        at = pl.ds(starts[i], chunks[i])
        green = [mine[side, :, at] + incoming[side, :, at].astype(F32) for side in range(2)]

        def pick(side, j, g):
            low = (j * groups + g) * rows
            return green[side][low : low + rows]

        for m in range(n_modes):
            chi = [
                (pick(0, j, 1 + m) * pick(1, j, 0) + pick(0, j, 0) * pick(1, j, 1 + m))
                .astype(BF16)
                .astype(F32)
                for j in range(n_time)
            ]
            for k in range(n_freq):
                total = None
                for j in range(n_time):
                    column = jnp.concatenate([columns[j, pl.ds(k, 1)]] * (chunks[i] // 128), axis=1)
                    term = (column * chi[j]).astype(BF16).astype(F32)
                    total = term if total is None else total + term
                out_ref[m, k, :, at] = total.astype(BF16)

    copies = []
    for i in range(n_chunk):
        copies.append(partial(i))
        if i > 0:
            copies[i - 1].wait_recv()
            finish(i - 1)
    copies[n_chunk - 1].wait_recv()
    finish(n_chunk - 1)
    for copy in sends + copies:
        copy.wait_send()


def shards(mesh, *args):
    (occ, occ_t, vir, vir_t, occ_e, occ_s, vir_e, vir_s, time_index, freq_index) = args
    n_tile, n_tm, n_orb = mesh.shape["tile"], mesh.shape["tm"], mesh.shape["orb"]
    n_modes = occ_t.shape[0]
    groups = 1 + n_modes
    n_occ, n_vir = occ.shape[1], vir.shape[1]
    n_time, n_freq = time_index.shape[0], freq_index.shape[0]
    points = occ.shape[0] // n_tm
    chunks = CHUNKS if points == sum(CHUNKS) else (points,)
    n_chunk = len(chunks)
    slab_rows = n_tile * SLAB_DEV
    rows = slab_rows // n_orb
    left_rows = n_time * groups * slab_rows
    half = left_rows // n_orb
    hbm = pl.BlockSpec(memory_space=pltpu.HBM)
    vmem = pl.BlockSpec(memory_space=pltpu.VMEM)
    smem = pltpu.SMEM
    dma = pltpu.SemaphoreType.DMA
    return pl.pallas_call(
        functools.partial(kernel, n_tile, chunks),
        out_shape=jax.ShapeDtypeStruct((n_modes, n_freq, rows, points), BF16),
        in_specs=[hbm] * 10,
        out_specs=vmem,
        scratch_shapes=[
            smem((n_time,), jnp.int32),
            smem((n_freq,), jnp.int32),
            pltpu.VMEM((n_occ,), F32),
            pltpu.VMEM((n_modes, n_occ), F32),
            pltpu.VMEM((n_vir,), F32),
            pltpu.VMEM((n_modes, n_vir), F32),
            pltpu.VMEM((n_time, groups, n_occ + n_vir), F32),
            pltpu.VMEM((n_time, n_freq, 128), F32),
            pltpu.VMEM((groups, points, n_occ), BF16),
            pltpu.VMEM((groups, points, n_vir), BF16),
            pltpu.VMEM((groups, 16, n_occ), BF16),
            pltpu.VMEM((groups, 16, n_vir), BF16),
            pltpu.VMEM((groups * SLAB_DEV, n_occ + n_vir), F32),
            pltpu.VMEM((n_tile, groups * SLAB_DEV, n_occ + n_vir), BF16),
            pltpu.VMEM((groups, slab_rows, n_occ + n_vir), F32),
            pltpu.VMEM((left_rows, groups * n_occ), BF16),
            pltpu.VMEM((left_rows, groups * n_vir), BF16),
            pltpu.VMEM((2, half, points), F32),
            pltpu.VMEM((2, half, points), BF16),
            pltpu.VMEM((2, half, points), BF16),
            dma((n_chunk, 4)),
            dma((4,)),
            dma((6,)),
            dma((n_tile - 1,)),
            dma((n_tile - 1,)),
            dma((n_chunk,)),
            dma((n_chunk,)),
        ],
        compiler_params=pltpu.CompilerParams(
            collective_id=0, has_side_effects=True, vmem_limit_bytes=56 * 1024 * 1024
        ),
        name="polarizability_tangent",
    )(time_index, freq_index, occ, occ_t, vir, vir_t, occ_e, occ_s, vir_e, vir_s)


def solution(mesh):
    in_specs = (
        P("tile", ("parts", "orb")),
        P(None, "tile", ("parts", "orb")),
        P("tile", ("parts", "orb")),
        P(None, "tile", ("parts", "orb")),
        P(("parts", "orb")),
        P(None, ("parts", "orb")),
        P(("parts", "orb")),
        P(None, ("parts", "orb")),
        P(),
        P(),
    )
    out_specs = P(None, None, ("parts", "orb"), ("tile", "tm"))
    return jax.shard_map(
        functools.partial(shards, mesh),
        mesh=mesh,
        in_specs=in_specs,
        out_specs=out_specs,
        check_vma=False,
    )
```
